32 devices in a mesh: cells: 8 (over z, core), tracer: 4 (over y, x).
Axes of the slice: x: 2, y: 2, z: 4, core: 2. Of those that a mesh axis runs over, the one named last changes fastest.
Arguments:
- adjoint: float32 [64, 32768], P('tracer', 'cells'), may hold values from -6 to 6
- blocks: float32 [1024, 128, 128], P('cells'), may hold values from -0.375 to 0.375
- row_ptr: int32 [8, 33], P('cells'), may hold values from 0 to 128, as said below
- col_idx: int32 [1024], P('cells'), may hold values from 0 to 255, as said below
- regime: int32 [256], P('cells'), may hold values from 0 to 7
- jac: float32 [8, 64, 64], replicated, as said below
Outputs:
- sensitivity: float32 [64, 32768], P('tracer', 'cells')
The draws below stay inside these ranges and needn't reach their ends.
Inputs may be any that keep to these rules, and one draw needn't show every extreme that they name: row_ptr[d, 0] = 0 and each block row holds 1 to 4 slots; some index of cells uses all 128 slots. `col_idx`: the first slot of each block row is its diagonal block; a live slot's column lies at most 32 blocks away from its block row, counted cyclically over the 256 blocks, and that distance is reached; slots past row_ptr[d, 32] hold any valid column. `jac`: each regime's matrix has diagonal entries of order one and off-diagonal couplings of order 0.1 between every pair of species.
All inputs are finite; a program needn't handle non-finite values.
Results may differ from the reference program's by a relative error of at most 0.0001.
Values sent between devices are 32-bit elements; how exact they have to be, the bound alone decides.
A program may use at most 64 MiB of HBM per device.

```python
import math
import jax
import jax.numpy as jnp
from jax import lax

SPEC = 64
BLOCK = 128
NB_DEV = 32
KMAX = 4
STEPS = 2
NREG = 8
NNZ_DEV = 128
NB = 256
NCELL = 32768


def sparsity_pattern(key):
    base = jax.random.fold_in(key, 11)
    key_level, key_full, key_count, key_sign, key_offset = jax.random.split(base, 5)
    device_count = NB // NB_DEV
    levels = jax.random.randint(key_level, (device_count,), 2, KMAX + 1)
    full_device = jax.random.randint(key_full, (), 0, device_count)
    raw_counts = jax.random.randint(key_count, (device_count, NB_DEV), 0, 1 << 20)
    row_counts = raw_counts % levels[:, None] + 1
    row_counts = jnp.where(jnp.arange(device_count)[:, None] == full_device, KMAX, row_counts)
    pointers = jnp.concatenate([jnp.zeros((device_count, 1), jnp.int32), jnp.cumsum(row_counts, axis=1).astype(jnp.int32)], axis=1)
    slot_ids = jnp.arange(NNZ_DEV).astype(jnp.int32)
    local_rows = jnp.sum((pointers[:, 1:, None] <= slot_ids[None, None, :]).astype(jnp.int32), axis=1)
    local_rows = jnp.minimum(local_rows, NB_DEV - 1)
    starts = jnp.take_along_axis(pointers, local_rows, axis=1)
    position = slot_ids[None, :] - starts
    signs = jax.random.randint(key_sign, (device_count, NNZ_DEV), 0, 2) * 2 - 1
    offsets = jax.random.randint(key_offset, (device_count, NNZ_DEV), -NB_DEV, NB_DEV + 1)
    offsets = jnp.where(position == 0, 0, jnp.where(position == 1, signs * NB_DEV, offsets))
    columns = jnp.mod(jnp.arange(device_count)[:, None] * NB_DEV + local_rows + offsets, NB)
    return (pointers.astype(jnp.int32), columns.reshape(-1).astype(jnp.int32))


def draw_row_ptr(key, part):
    pointers, columns = sparsity_pattern(key)
    return pointers


def draw_col_idx(key, part):
    pointers, columns = sparsity_pattern(key)
    return columns


def draw_jac(key, part):
    key_diag, key_coupling = jax.random.split(jax.random.fold_in(key, 23))
    diagonal = jax.random.uniform(key_diag, (NREG, SPEC), jnp.float32, 0.6, 1.1)
    coupling = jax.random.normal(key_coupling, (NREG, SPEC, SPEC), jnp.float32) * (0.6 / math.sqrt(SPEC))
    return coupling + diagonal[:, :, None] * jnp.eye(SPEC, dtype=jnp.float32)[None, :, :]


def with_ends(values, own_key, low, top_value):
    index_at = [jax.random.randint(jax.random.fold_in(own_key, axis), (), 0, length) for axis, length in enumerate(values.shape)]
    longest = values.shape.index(max(values.shape))
    neighbour = index_at[:longest] + [(index_at[longest] + 1) % values.shape[longest]] + index_at[longest + 1:]
    return values.at[tuple(index_at)].set(low).at[tuple(neighbour)].set(top_value)


def shard_levels(stream_key, extent, cuts, low, top_value):
    gain = 1.0
    for dim, shards_of in cuts:
        steps = jax.random.uniform(jax.random.fold_in(jax.random.fold_in(stream_key, 6), dim), (shards_of,), jnp.float32, low / len(cuts), top_value / len(cuts))
        gain = gain * jnp.repeat(jnp.exp(steps), extent[dim] // shards_of).reshape((-1,) + (1,) * (len(extent) - 1 - dim))
    return gain


def normal_values(rng, extent, width, most, shards=(), kind=jnp.bfloat16):
    drawn = width * jax.random.normal(rng, extent, jnp.float32)
    if shards:
        drawn = drawn * shard_levels(rng, extent, shards, -0.22, 0.18)
    return jnp.clip(drawn, -most, most).astype(kind)


def setup_inputs(seed: int = 0) -> dict:
    key_of = jax.random.split(jax.random.key(seed), 7)
    return {
        "adjoint": normal_values(key_of[0], (SPEC, NCELL), 1.0, 6.0, ((0, 4), (1, 8)), jnp.float32),
        "blocks": normal_values(key_of[1], (NB * KMAX, BLOCK, BLOCK), (2 * BLOCK) ** -0.5, 0.375, ((0, 8),), jnp.float32),
        "row_ptr": draw_row_ptr(jax.random.fold_in(key_of[6], 71), 0),
        "col_idx": draw_col_idx(jax.random.fold_in(key_of[6], 71), 0),
        "regime": with_ends(jax.random.randint(key_of[4], (NB,), 0, NREG), jax.random.fold_in(key_of[4], 1), 0, NREG - 1).astype(jnp.int32),
        "jac": draw_jac(jax.random.fold_in(key_of[6], 71), 0),
    }


def chemistry(moved, cell_regime, jac):
    result = jnp.zeros(moved.shape, jnp.float32)
    for regime_id in range(jac.shape[0]):
        reacted = jnp.einsum('ts,tc->sc', jac[regime_id], moved, precision=lax.Precision.HIGHEST)
        result = result + jnp.where(cell_regime[None, :] == regime_id, reacted, jnp.zeros_like(reacted))
    return result


def reference(adjoint, blocks, row_ptr, col_idx, regime, jac):
    device_count = NB // NB_DEV
    slot_ids = jnp.arange(NNZ_DEV).astype(jnp.int32)
    local_rows = jnp.sum((row_ptr[:, 1:, None] <= slot_ids[None, None, :]).astype(jnp.int32), axis=1)
    occupied = slot_ids[None, :] < row_ptr[:, -1:]
    global_rows = jnp.arange(device_count).astype(jnp.int32)[:, None] * NB_DEV + local_rows
    global_rows = jnp.where(occupied, global_rows, NB).reshape(-1)
    cell_regime = jnp.repeat(regime, BLOCK)
    adjoint_field = adjoint
    for hour_step in range(STEPS):
        gathered = adjoint_field.reshape(SPEC, NB, BLOCK)[:, col_idx, :]
        products = jnp.einsum('sij,qsj->sqi', blocks, gathered, precision=lax.Precision.HIGHEST)
        summed = jax.ops.segment_sum(products, global_rows, num_segments=NB)
        moved = jnp.transpose(summed, (1, 0, 2)).reshape(SPEC, NCELL)
        adjoint_field = chemistry(moved, cell_regime, jac)
    return adjoint_field
```

```python
import functools

import jax
import jax.numpy as jnp
from jax import lax
from jax.experimental import pallas as pl
from jax.experimental.pallas import tpu as pltpu
from jax.sharding import PartitionSpec as P

BLOCK = 128
STEPS = 2
KMAX = 4
CHUNKS = 8
UNROLL = 4


def split(v):
    high = v.astype(jnp.bfloat16).astype(jnp.float32)
    return high, v - high


def kernel(n_cells, n_tracer, row_ptr, col_idx, regime, adjoint, blocks, jac, out,
           raw, weights, jt, ext, halves, sent, arrived, back,
           raw_sem, near_sem, first_send, first_recv, to_send, to_recv,
           back_send, back_recv, halo_send, halo_recv, out_sem):
    spec, cells = adjoint.shape
    slots = blocks.shape[0]
    nb = cells // BLOCK
    rows = nb // n_tracer
    part = cells // n_tracer
    nb_total = nb * n_cells
    d = lax.axis_index("cells")
    t = lax.axis_index("tracer")
    right = lax.rem(d + 1, n_cells)
    left = lax.rem(d + n_cells - 1, n_cells)

    per = slots // CHUNKS
    raw_copies = [
        pltpu.make_async_copy(blocks.at[pl.ds(c * per, per)], raw.at[pl.ds(c * per, per)], raw_sem.at[c])
        for c in range(CHUNKS)
    ]

    barrier = pltpu.get_barrier_semaphore()
    pl.semaphore_signal(barrier, inc=1, device_id={"cells": left}, device_id_type=pl.DeviceIdType.MESH)
    pl.semaphore_signal(barrier, inc=1, device_id={"cells": right}, device_id_type=pl.DeviceIdType.MESH)
    for p in range(1, n_tracer):
        pl.semaphore_signal(barrier, inc=1, device_id={"tracer": lax.rem(t + p, n_tracer)},
                            device_id_type=pl.DeviceIdType.MESH)
    near = pltpu.make_async_copy(adjoint, ext.at[0, :, pl.ds(cells, cells)], near_sem)
    near.start()
    for copy in raw_copies:
        copy.start()
    pl.semaphore_wait(barrier, n_tracer + 1)

    def remote(src, dst, send, recv, where):
        return pltpu.make_async_remote_copy(
            src_ref=src, dst_ref=dst, send_sem=send, recv_sem=recv,
            device_id=where, device_id_type=pl.DeviceIdType.MESH)

    first = [
        remote(adjoint, ext.at[0, :, pl.ds(0, cells)], first_send.at[0], first_recv.at[0], {"cells": right}),
        remote(adjoint, ext.at[0, :, pl.ds(2 * cells, cells)], first_send.at[1], first_recv.at[1], {"cells": left}),
    ]
    for copy in first:
        copy.start()

    for r in range(jac.shape[0]):
        high, low = split(jnp.transpose(jac[r]))
        jt[r] = jnp.concatenate([high, low], axis=0).astype(jnp.bfloat16)
    for c in range(CHUNKS):
        raw_copies[c].wait()

        def prepare(s, carry):
            high, low = split(raw[s])
            weights[s, 0:BLOCK] = high.astype(jnp.bfloat16)
            weights[s, BLOCK:2 * BLOCK] = low.astype(jnp.bfloat16)
            return carry

        lax.fori_loop(c * per, (c + 1) * per, prepare, 0, unroll=2)

    def take_in(step, begin, count):
        def one(i, carry):
            g = begin + i
            high, low = split(ext[step, :, pl.ds(pl.multiple_of(g * BLOCK, BLOCK), BLOCK)])
            halves[g] = jnp.concatenate([high, low], axis=0).astype(jnp.bfloat16)
            return carry

        lax.fori_loop(0, count, one, 0, unroll=min(UNROLL, count))

    halves[3 * nb] = jnp.zeros((2 * spec, BLOCK), jnp.bfloat16)
    near.wait()
    take_in(0, nb, nb)
    for copy, third in zip(first, (0, 2)):
        copy.wait_recv()
        take_in(0, third * nb, nb)

    def moved_row(row):
        begin = row_ptr[0, row]
        end = row_ptr[0, row + 1]
        xs, ws = [], []
        for k in range(KMAX):
            live = begin + k < end
            slot = jnp.minimum(begin + k, slots - 1)
            column = col_idx[slot] - (d - 1) * nb
            column = jnp.where(column < 0, column + nb_total, column)
            column = jnp.where(column >= nb_total, column - nb_total, column)
            column = jnp.where(live, jnp.clip(column, 0, 3 * nb - 1), 3 * nb)
            xs.append(halves[column])
            ws.append(weights[slot])
        lhs = jnp.concatenate(xs, axis=1)
        got = lax.dot_general(lhs, jnp.concatenate(ws, axis=1), (((1,), (1,)), ((), ())),
                              preferred_element_type=jnp.float32)
        got = got[:, 0:BLOCK] + got[:, BLOCK:2 * BLOCK]
        return got[0:spec] + got[spec:2 * spec]

    pending = list(first)
    for step in range(STEPS):
        to = []
        for p in list(range(1, n_tracer)) + [0]:
            owner = lax.rem(t + p, n_tracer)

            def transport(i, carry, p=p, owner=owner):
                y = moved_row(owner * rows + i)
                where = pl.ds(pl.multiple_of(i * BLOCK, BLOCK), BLOCK)
                if p:
                    sent[step, p, :, where] = y
                else:
                    arrived[step, t, :, where] = y
                return carry

            lax.fori_loop(0, rows, transport, 0, unroll=min(UNROLL, rows))
            if p:
                copy = remote(sent.at[step, p], arrived.at[step, t], to_send.at[step, p],
                              to_recv.at[step, p], {"tracer": owner})
                copy.start()
                to.append(copy)
        for copy in to:
            copy.wait_recv()
        pending += to

        last = step == STEPS - 1
        for b in range(rows):
            cols = pl.ds(b * BLOCK, BLOCK)
            m = jnp.concatenate([arrived[step, q, :, cols] for q in range(n_tracer)], axis=0)
            high, low = split(m)
            got = lax.dot_general(jt[regime[t * rows + b]],
                                  jnp.concatenate([high, low], axis=1).astype(jnp.bfloat16),
                                  (((1,), (0,)), ((), ())), preferred_element_type=jnp.float32)
            got = got[:, 0:BLOCK] + got[:, BLOCK:2 * BLOCK]
            half = got.shape[0] // 2
            got = got[0:half] + got[half:]
            for q in range(n_tracer):
                back[step, q, :, cols] = got[q * spec:(q + 1) * spec]

        mine = pl.ds(pl.multiple_of(t * part, BLOCK), part)
        centre = pl.ds(pl.multiple_of(cells + t * part, BLOCK), part)
        returned = []
        for p in range(1, n_tracer):
            q = lax.rem(t + p, n_tracer)
            target = out.at[:, mine] if last else ext.at[step + 1, :, centre]
            copy = remote(back.at[step, q], target, back_send.at[step, p], back_recv.at[step, p], {"tracer": q})
            copy.start()
            returned.append(copy)
        pending += returned
        if last:
            own = pltpu.make_async_copy(back.at[step, t], out.at[:, mine], out_sem)
            own.start()
            for copy in returned:
                copy.wait_recv()
            own.wait()
        else:
            ext[step + 1, :, centre] = back[step, t]
            halo = []
            for p in range(n_tracer):
                q = lax.rem(t + n_tracer - p, n_tracer)
                if p:
                    returned[p - 1].wait_recv()

                def place(third, q=q):
                    return ext.at[step + 1, :, pl.ds(pl.multiple_of(third * cells + q * part, BLOCK), part)]

                for side, (third, where) in enumerate(((0, right), (2, left))):
                    copy = remote(place(1), place(third), halo_send.at[step, side, p],
                                  halo_recv.at[step, side, p], {"cells": where})
                    copy.start()
                    halo.append((copy, third * nb + q * rows))
                take_in(step + 1, nb + q * rows, rows)
            for copy, begin in halo:
                copy.wait_recv()
                take_in(step + 1, begin, rows)
            pending += [copy for copy, _ in halo]
    for copy in pending:
        copy.wait_send()


def body(adjoint, blocks, row_ptr, col_idx, regime, jac, n_cells, n_tracer):
    spec, cells = adjoint.shape
    slots = blocks.shape[0]
    part = cells // n_tracer
    f32, bf16 = jnp.float32, jnp.bfloat16
    dma = pltpu.SemaphoreType.DMA
    smem = pl.BlockSpec(memory_space=pltpu.SMEM)
    return pl.pallas_call(
        functools.partial(kernel, n_cells, n_tracer),
        out_shape=jax.ShapeDtypeStruct((spec, cells), f32),
        in_specs=[smem, smem, smem,
                  pl.BlockSpec(memory_space=pl.ANY), pl.BlockSpec(memory_space=pl.ANY),
                  pl.BlockSpec(memory_space=pltpu.VMEM)],
        out_specs=pl.BlockSpec(memory_space=pl.ANY),
        scratch_shapes=[
            pltpu.VMEM((slots, BLOCK, BLOCK), f32),
            pltpu.VMEM((slots, 2 * BLOCK, BLOCK), bf16),
            pltpu.VMEM((jac.shape[0], 2 * jac.shape[2], jac.shape[1]), bf16),
            pltpu.VMEM((STEPS, spec, 3 * cells), f32),
            pltpu.VMEM((3 * cells // BLOCK + 1, 2 * spec, BLOCK), bf16),
            pltpu.VMEM((STEPS, n_tracer, spec, part), f32),
            pltpu.VMEM((STEPS, n_tracer, spec, part), f32),
            pltpu.VMEM((STEPS, n_tracer, spec, part), f32),
            dma((CHUNKS,)), dma(()), dma((2,)), dma((2,)),
            dma((STEPS, n_tracer)), dma((STEPS, n_tracer)),
            dma((STEPS, n_tracer)), dma((STEPS, n_tracer)),
            dma((STEPS, 2, n_tracer)), dma((STEPS, 2, n_tracer)), dma(()),
        ],
        compiler_params=pltpu.CompilerParams(
            collective_id=0, has_side_effects=True, vmem_limit_bytes=40 * 2**20),
    )(row_ptr, col_idx, regime, adjoint, blocks, jac)


def solution(mesh):
    return jax.shard_map(
        functools.partial(body, n_cells=mesh.shape["cells"], n_tracer=mesh.shape["tracer"]),
        mesh=mesh,
        in_specs=(
            P("tracer", "cells"),
            P("cells", None, None),
            P("cells", None),
            P("cells"),
            P("cells"),
            P(),
        ),
        out_specs=P("tracer", "cells"),
        check_vma=False,
    )
```

```python
import functools

import jax
import jax.numpy as jnp
from jax import lax
from jax.experimental import pallas as pl
from jax.experimental.pallas import tpu as pltpu
from jax.sharding import PartitionSpec as P

BLOCK = 128
STEPS = 2
KMAX = 4
CHUNKS = 8
UNROLL = 4


def split(v):
    high = v.astype(jnp.bfloat16).astype(jnp.float32)
    return high, v - high


def kernel(n_cells, n_tracer, row_ptr_hbm, col_idx_hbm, regime_hbm, adjoint, blocks, jac_hbm, out,
           row_ptr, col_idx, regime, jac, raw, weights, jt, ext, halves, sent, arrived, back,
           raw_sem, near_sem, first_send, first_recv, to_send, to_recv,
           back_send, back_recv, halo_send, halo_recv, out_sem, small_sem):
    spec, cells = adjoint.shape
    slots = blocks.shape[0]
    nb = cells // BLOCK
    rows = nb // n_tracer
    part = cells // n_tracer
    nb_total = nb * n_cells
    d = lax.axis_index("cells")
    t = lax.axis_index("tracer")
    right = lax.rem(d + 1, n_cells)
    left = lax.rem(d + n_cells - 1, n_cells)

    per = slots // CHUNKS
    raw_copies = [
        pltpu.make_async_copy(blocks.at[pl.ds(c * per, per)], raw.at[pl.ds(c * per, per)], raw_sem.at[c])
        for c in range(CHUNKS)
    ]

    barrier = pltpu.get_barrier_semaphore()
    pl.semaphore_signal(barrier, inc=1, device_id={"cells": left}, device_id_type=pl.DeviceIdType.MESH)
    pl.semaphore_signal(barrier, inc=1, device_id={"cells": right}, device_id_type=pl.DeviceIdType.MESH)
    for p in range(1, n_tracer):
        pl.semaphore_signal(barrier, inc=1, device_id={"tracer": lax.rem(t + p, n_tracer)},
                            device_id_type=pl.DeviceIdType.MESH)
    near = pltpu.make_async_copy(adjoint, ext.at[0, :, pl.ds(cells, cells)], near_sem)
    near.start()
    small = [
        pltpu.make_async_copy(source, here, small_sem.at[i])
        for i, (source, here) in enumerate(
            ((row_ptr_hbm, row_ptr), (col_idx_hbm, col_idx), (regime_hbm, regime), (jac_hbm, jac)))
    ]
    for copy in small:
        copy.start()
    for copy in raw_copies:
        copy.start()
    pl.semaphore_wait(barrier, n_tracer + 1)

    def remote(src, dst, send, recv, where):
        return pltpu.make_async_remote_copy(
            src_ref=src, dst_ref=dst, send_sem=send, recv_sem=recv,
            device_id=where, device_id_type=pl.DeviceIdType.MESH)

    first = [
        remote(adjoint, ext.at[0, :, pl.ds(0, cells)], first_send.at[0], first_recv.at[0], {"cells": right}),
        remote(adjoint, ext.at[0, :, pl.ds(2 * cells, cells)], first_send.at[1], first_recv.at[1], {"cells": left}),
    ]
    for copy in first:
        copy.start()

    for copy in small:
        copy.wait()
    for r in range(jac.shape[0]):
        high, low = split(jnp.transpose(jac[r]))
        jt[r] = jnp.concatenate([high, low], axis=0).astype(jnp.bfloat16)
    for c in range(CHUNKS):
        raw_copies[c].wait()

        def prepare(s, carry):
            high, low = split(raw[s])
            weights[s, 0:BLOCK] = high.astype(jnp.bfloat16)
            weights[s, BLOCK:2 * BLOCK] = low.astype(jnp.bfloat16)
            return carry

        lax.fori_loop(c * per, (c + 1) * per, prepare, 0, unroll=2)

    def take_in(step, begin, count):
        def one(i, carry):
            g = begin + i
            high, low = split(ext[step, :, pl.ds(pl.multiple_of(g * BLOCK, BLOCK), BLOCK)])
            halves[g] = jnp.concatenate([high, low], axis=0).astype(jnp.bfloat16)
            return carry

        lax.fori_loop(0, count, one, 0, unroll=min(UNROLL, count))

    halves[3 * nb] = jnp.zeros((2 * spec, BLOCK), jnp.bfloat16)
    near.wait()
    take_in(0, nb, nb)
    for copy, third in zip(first, (0, 2)):
        copy.wait_recv()
        take_in(0, third * nb, nb)

    def moved_row(row):
        begin = row_ptr[0, row]
        end = row_ptr[0, row + 1]
        xs, ws = [], []
        for k in range(KMAX):
            live = begin + k < end
            slot = jnp.minimum(begin + k, slots - 1)
            column = col_idx[slot] - (d - 1) * nb
            column = jnp.where(column < 0, column + nb_total, column)
            column = jnp.where(column >= nb_total, column - nb_total, column)
            column = jnp.where(live, jnp.clip(column, 0, 3 * nb - 1), 3 * nb)
            xs.append(halves[column])
            ws.append(weights[slot])
        lhs = jnp.concatenate(xs, axis=1)
        got = lax.dot_general(lhs, jnp.concatenate(ws, axis=1), (((1,), (1,)), ((), ())),
                              preferred_element_type=jnp.float32)
        got = got[:, 0:BLOCK] + got[:, BLOCK:2 * BLOCK]
        return got[0:spec] + got[spec:2 * spec]

    pending = list(first)
    for step in range(STEPS):
        to = []
        for p in list(range(1, n_tracer)) + [0]:
            owner = lax.rem(t + p, n_tracer)

            def transport(i, carry, p=p, owner=owner):
                y = moved_row(owner * rows + i)
                where = pl.ds(pl.multiple_of(i * BLOCK, BLOCK), BLOCK)
                if p:
                    sent[step, p, :, where] = y
                else:
                    arrived[step, t, :, where] = y
                return carry

            lax.fori_loop(0, rows, transport, 0, unroll=min(UNROLL, rows))
            if p:
                copy = remote(sent.at[step, p], arrived.at[step, t], to_send.at[step, p],
                              to_recv.at[step, p], {"tracer": owner})
                copy.start()
                to.append(copy)
        for copy in to:
            copy.wait_recv()
        pending += to

        last = step == STEPS - 1
        for b in range(rows):
            cols = pl.ds(b * BLOCK, BLOCK)
            m = jnp.concatenate([arrived[step, q, :, cols] for q in range(n_tracer)], axis=0)
            high, low = split(m)
            got = lax.dot_general(jt[regime[t * rows + b]],
                                  jnp.concatenate([high, low], axis=1).astype(jnp.bfloat16),
                                  (((1,), (0,)), ((), ())), preferred_element_type=jnp.float32)
            got = got[:, 0:BLOCK] + got[:, BLOCK:2 * BLOCK]
            half = got.shape[0] // 2
            got = got[0:half] + got[half:]
            for q in range(n_tracer):
                back[step, q, :, cols] = got[q * spec:(q + 1) * spec]

        mine = pl.ds(pl.multiple_of(t * part, BLOCK), part)
        centre = pl.ds(pl.multiple_of(cells + t * part, BLOCK), part)
        returned = []
        for p in range(1, n_tracer):
            q = lax.rem(t + p, n_tracer)
            target = out.at[:, mine] if last else ext.at[step + 1, :, centre]
            copy = remote(back.at[step, q], target, back_send.at[step, p], back_recv.at[step, p], {"tracer": q})
            copy.start()
            returned.append(copy)
        pending += returned
        if last:
            own = pltpu.make_async_copy(back.at[step, t], out.at[:, mine], out_sem)
            own.start()
            for copy in returned:
                copy.wait_recv()
            own.wait()
        else:
            ext[step + 1, :, centre] = back[step, t]
            halo = []
            for p in range(n_tracer):
                q = lax.rem(t + n_tracer - p, n_tracer)
                if p:
                    returned[p - 1].wait_recv()

                def place(third, q=q):
                    return ext.at[step + 1, :, pl.ds(pl.multiple_of(third * cells + q * part, BLOCK), part)]

                for side, (third, where) in enumerate(((0, right), (2, left))):
                    copy = remote(place(1), place(third), halo_send.at[step, side, p],
                                  halo_recv.at[step, side, p], {"cells": where})
                    copy.start()
                    halo.append((copy, third * nb + q * rows))
                take_in(step + 1, nb + q * rows, rows)
            for copy, begin in halo:
                copy.wait_recv()
                take_in(step + 1, begin, rows)
            pending += [copy for copy, _ in halo]
    for copy in pending:
        copy.wait_send()


def body(adjoint, blocks, row_ptr, col_idx, regime, jac, n_cells, n_tracer):
    spec, cells = adjoint.shape
    slots = blocks.shape[0]
    part = cells // n_tracer
    f32, bf16 = jnp.float32, jnp.bfloat16
    dma = pltpu.SemaphoreType.DMA
    return pl.pallas_call(
        functools.partial(kernel, n_cells, n_tracer),
        out_shape=jax.ShapeDtypeStruct((spec, cells), f32),
        in_specs=[pl.BlockSpec(memory_space=pl.ANY)] * 6,
        out_specs=pl.BlockSpec(memory_space=pl.ANY),
        scratch_shapes=[
            pltpu.SMEM(row_ptr.shape, row_ptr.dtype),
            pltpu.SMEM(col_idx.shape, col_idx.dtype),
            pltpu.SMEM(regime.shape, regime.dtype),
            pltpu.VMEM(jac.shape, f32),
            pltpu.VMEM((slots, BLOCK, BLOCK), f32),
            pltpu.VMEM((slots, 2 * BLOCK, BLOCK), bf16),
            pltpu.VMEM((jac.shape[0], 2 * jac.shape[2], jac.shape[1]), bf16),
            pltpu.VMEM((STEPS, spec, 3 * cells), f32),
            pltpu.VMEM((3 * cells // BLOCK + 1, 2 * spec, BLOCK), bf16),
            pltpu.VMEM((STEPS, n_tracer, spec, part), f32),
            pltpu.VMEM((STEPS, n_tracer, spec, part), f32),
            pltpu.VMEM((STEPS, n_tracer, spec, part), f32),
            dma((CHUNKS,)), dma(()), dma((2,)), dma((2,)),
            dma((STEPS, n_tracer)), dma((STEPS, n_tracer)),
            dma((STEPS, n_tracer)), dma((STEPS, n_tracer)),
            dma((STEPS, 2, n_tracer)), dma((STEPS, 2, n_tracer)), dma(()), dma((4,)),
        ],
        compiler_params=pltpu.CompilerParams(
            collective_id=0, has_side_effects=True, vmem_limit_bytes=60 * 2**20),
    )(row_ptr, col_idx, regime, adjoint, blocks, jac)


def solution(mesh):
    return jax.shard_map(
        functools.partial(body, n_cells=mesh.shape["cells"], n_tracer=mesh.shape["tracer"]),
        mesh=mesh,
        in_specs=(
            P("tracer", "cells"),
            P("cells", None, None),
            P("cells", None),
            P("cells"),
            P("cells"),
            P(),
        ),
        out_specs=P("tracer", "cells"),
        check_vma=False,
    )
```

```python
import functools
import math

import jax
import jax.numpy as jnp
from jax import lax
from jax.experimental import pallas as pl
from jax.experimental.pallas import tpu as pltpu
from jax.sharding import PartitionSpec as P

BLOCK = 128
STEPS = 2
KMAX = 4
CHUNKS = 8
UNROLL = 4
PIECES = 2
HALO = 4


def split(v):
    high = v.astype(jnp.bfloat16).astype(jnp.float32)
    return high, v - high


def kernel(n_cells, n_tracer, row_ptr_hbm, col_idx_hbm, regime_hbm, adjoint, blocks, jac_hbm, out,
           row_ptr, col_idx, regime, jac, raw, weights, jt, ext, halves, sent, arrived, back,
           raw_sem, near_sem, first_send, first_recv, to_send, to_recv,
           back_send, back_recv, halo_send, halo_recv, out_sem, small_sem):
    spec, cells = adjoint.shape
    slots = blocks.shape[0]
    nb = cells // BLOCK
    rows = nb // n_tracer
    part = cells // n_tracer
    nb_total = nb * n_cells
    pieces = arrived.shape[1]
    piece = part // pieces
    piece_rows = rows // pieces
    d = lax.axis_index("cells")
    t = lax.axis_index("tracer")
    right = lax.rem(d + 1, n_cells)
    left = lax.rem(d + n_cells - 1, n_cells)

    per = slots // CHUNKS
    raw_copies = [
        pltpu.make_async_copy(blocks.at[pl.ds(c * per, per)], raw.at[pl.ds(c * per, per)], raw_sem.at[c])
        for c in range(CHUNKS)
    ]

    barrier = pltpu.get_barrier_semaphore()
    pl.semaphore_signal(barrier, inc=1, device_id={"cells": left}, device_id_type=pl.DeviceIdType.MESH)
    pl.semaphore_signal(barrier, inc=1, device_id={"cells": right}, device_id_type=pl.DeviceIdType.MESH)
    for p in range(1, n_tracer):
        pl.semaphore_signal(barrier, inc=1, device_id={"tracer": lax.rem(t + p, n_tracer)},
                            device_id_type=pl.DeviceIdType.MESH)
    near = pltpu.make_async_copy(adjoint, ext.at[0, :, pl.ds(cells, cells)], near_sem)
    near.start()
    small = [
        pltpu.make_async_copy(source, here, small_sem.at[i])
        for i, (source, here) in enumerate(
            ((row_ptr_hbm, row_ptr), (col_idx_hbm, col_idx), (regime_hbm, regime), (jac_hbm, jac)))
    ]
    for copy in small:
        copy.start()
    pl.semaphore_wait(barrier, n_tracer + 1)

    def remote(src, dst, send, recv, where):
        return pltpu.make_async_remote_copy(
            src_ref=src, dst_ref=dst, send_sem=send, recv_sem=recv,
            device_id=where, device_id_type=pl.DeviceIdType.MESH)

    near.wait()
    wide = cells // HALO
    first = [
        remote(ext.at[0, :, pl.ds(cells + g * wide, wide)], ext.at[0, :, pl.ds(third * cells + g * wide, wide)],
               first_send.at[side, g], first_recv.at[side, g], {"cells": where})
        for g in range(HALO) for side, (third, where) in enumerate(((0, right), (2, left)))
    ]
    for copy in first:
        copy.start()
    for copy in raw_copies:
        copy.start()

    for copy in small:
        copy.wait()
    for r in range(jac.shape[0]):
        high, low = split(jnp.transpose(jac[r]))
        jt[r] = jnp.concatenate([high, low], axis=0).astype(jnp.bfloat16)
    for c in range(CHUNKS):
        raw_copies[c].wait()

        def prepare(s, carry):
            high, low = split(raw[s])
            weights[s, 0:BLOCK] = high.astype(jnp.bfloat16)
            weights[s, BLOCK:2 * BLOCK] = low.astype(jnp.bfloat16)
            return carry

        lax.fori_loop(c * per, (c + 1) * per, prepare, 0, unroll=2)

    def take_in(step, begin, count):
        def one(i, carry):
            g = begin + i
            high, low = split(ext[step, :, pl.ds(pl.multiple_of(g * BLOCK, BLOCK), BLOCK)])
            halves[g] = jnp.concatenate([high, low], axis=0).astype(jnp.bfloat16)
            return carry

        lax.fori_loop(0, count, one, 0, unroll=min(UNROLL, count))

    halves[3 * nb] = jnp.zeros((2 * spec, BLOCK), jnp.bfloat16)
    take_in(0, nb, nb)
    for i, copy in enumerate(first):
        copy.wait_recv()
        take_in(0, (i % 2) * 2 * nb + (i // 2) * (nb // HALO), nb // HALO)

    def moved_row(row):
        begin = row_ptr[0, row]
        end = row_ptr[0, row + 1]
        xs, ws = [], []
        for k in range(KMAX):
            live = begin + k < end
            slot = jnp.minimum(begin + k, slots - 1)
            column = col_idx[slot] - (d - 1) * nb
            column = jnp.where(column < 0, column + nb_total, column)
            column = jnp.where(column >= nb_total, column - nb_total, column)
            column = jnp.where(live, jnp.clip(column, 0, 3 * nb - 1), 3 * nb)
            xs.append(halves[column])
            ws.append(weights[slot])
        lhs = jnp.concatenate(xs, axis=1)
        got = lax.dot_general(lhs, jnp.concatenate(ws, axis=1), (((1,), (1,)), ((), ())),
                              preferred_element_type=jnp.float32)
        got = got[:, 0:BLOCK] + got[:, BLOCK:2 * BLOCK]
        return got[0:spec] + got[spec:2 * spec]

    pending = list(first)
    peers = range(1, n_tracer)
    for step in range(STEPS):
        to = {}
        for h in range(pieces):
            for p in (*peers, 0):
                owner = lax.rem(t + p, n_tracer)

                def transport(i, carry, p=p, h=h, owner=owner):
                    y = moved_row(owner * rows + h * piece_rows + i)
                    where = pl.ds(pl.multiple_of(i * BLOCK, BLOCK), BLOCK)
                    if p:
                        sent[step, h, p, :, where] = y
                    else:
                        arrived[step, h, t, :, where] = y
                    return carry

                lax.fori_loop(0, piece_rows, transport, 0, unroll=min(UNROLL, piece_rows))
                if p:
                    to[h, p] = remote(sent.at[step, h, p], arrived.at[step, h, t], to_send.at[step, h, p],
                                      to_recv.at[step, h, p], {"tracer": owner})
                    to[h, p].start()

        last = step == STEPS - 1
        returned, halo = {}, []

        def place(third, q, h):
            start = third * cells + q * part + h * piece
            return ext.at[step + 1, :, pl.ds(pl.multiple_of(start, BLOCK), piece)]

        def forward(p, h):
            q = lax.rem(t + n_tracer - p, n_tracer)
            for side, (third, where) in enumerate(((0, right), (2, left))):
                copy = remote(place(1, q, h), place(third, q, h), halo_send.at[step, side, h, p],
                              halo_recv.at[step, side, h, p], {"cells": where})
                copy.start()
                halo.append((copy, third * nb + q * rows + h * piece_rows))

        for h in range(pieces):
            for p in peers:
                to[h, p].wait_recv()
            for b in range(piece_rows):
                cols = pl.ds(b * BLOCK, BLOCK)
                m = jnp.concatenate([arrived[step, h, q, :, cols] for q in range(n_tracer)], axis=0)
                high, low = split(m)
                got = lax.dot_general(jt[regime[t * rows + h * piece_rows + b]],
                                      jnp.concatenate([high, low], axis=1).astype(jnp.bfloat16),
                                      (((1,), (0,)), ((), ())), preferred_element_type=jnp.float32)
                got = got[:, 0:BLOCK] + got[:, BLOCK:2 * BLOCK]
                half = got.shape[0] // 2
                got = got[0:half] + got[half:]
                for q in range(n_tracer):
                    back[step, h, q, :, cols] = got[q * spec:(q + 1) * spec]

            mine = pl.ds(pl.multiple_of(t * part + h * piece, BLOCK), piece)
            for p in peers:
                q = lax.rem(t + p, n_tracer)
                target = out.at[:, mine] if last else place(1, t, h)
                returned[h, p] = remote(back.at[step, h, q], target, back_send.at[step, h, p],
                                        back_recv.at[step, h, p], {"tracer": q})
                returned[h, p].start()
            if last:
                pltpu.make_async_copy(back.at[step, h, t], out.at[:, mine], out_sem.at[h]).start()
            else:
                ext[step + 1, :, pl.ds(pl.multiple_of(cells + t * part + h * piece, BLOCK), piece)] = back[step, h, t]
                forward(0, h)
                take_in(step + 1, nb + t * rows + h * piece_rows, piece_rows)
        for h in range(pieces):
            for p in peers:
                returned[h, p].wait_recv()
                if not last:
                    forward(p, h)
                    q = lax.rem(t + n_tracer - p, n_tracer)
                    take_in(step + 1, nb + q * rows + h * piece_rows, piece_rows)
            if last:
                mine = pl.ds(pl.multiple_of(t * part + h * piece, BLOCK), piece)
                pltpu.make_async_copy(back.at[step, h, t], out.at[:, mine], out_sem.at[h]).wait()
        for copy, begin in halo:
            copy.wait_recv()
            take_in(step + 1, begin, piece_rows)
        pending += [*to.values(), *returned.values(), *(copy for copy, _ in halo)]
    for copy in pending:
        copy.wait_send()


def body(adjoint, blocks, row_ptr, col_idx, regime, jac, n_cells, n_tracer):
    spec, cells = adjoint.shape
    slots = blocks.shape[0]
    part = cells // n_tracer
    pieces = math.gcd(PIECES, part // BLOCK)
    f32, bf16 = jnp.float32, jnp.bfloat16
    dma = pltpu.SemaphoreType.DMA
    return pl.pallas_call(
        functools.partial(kernel, n_cells, n_tracer),
        out_shape=jax.ShapeDtypeStruct((spec, cells), f32),
        in_specs=[pl.BlockSpec(memory_space=pl.ANY)] * 6,
        out_specs=pl.BlockSpec(memory_space=pl.ANY),
        scratch_shapes=[
            pltpu.SMEM(row_ptr.shape, row_ptr.dtype),
            pltpu.SMEM(col_idx.shape, col_idx.dtype),
            pltpu.SMEM(regime.shape, regime.dtype),
            pltpu.VMEM(jac.shape, f32),
            pltpu.VMEM((slots, BLOCK, BLOCK), f32),
            pltpu.VMEM((slots, 2 * BLOCK, BLOCK), bf16),
            pltpu.VMEM((jac.shape[0], 2 * jac.shape[2], jac.shape[1]), bf16),
            pltpu.VMEM((STEPS, spec, 3 * cells), f32),
            pltpu.VMEM((3 * cells // BLOCK + 1, 2 * spec, BLOCK), bf16),
            pltpu.VMEM((STEPS, pieces, n_tracer, spec, part // pieces), f32),
            pltpu.VMEM((STEPS, pieces, n_tracer, spec, part // pieces), f32),
            pltpu.VMEM((STEPS, pieces, n_tracer, spec, part // pieces), f32),
            dma((CHUNKS,)), dma(()), dma((2, HALO)), dma((2, HALO)),
            dma((STEPS, pieces, n_tracer)), dma((STEPS, pieces, n_tracer)),
            dma((STEPS, pieces, n_tracer)), dma((STEPS, pieces, n_tracer)),
            dma((STEPS, 2, pieces, n_tracer)), dma((STEPS, 2, pieces, n_tracer)), dma((pieces,)), dma((4,)),
        ],
        compiler_params=pltpu.CompilerParams(
            collective_id=0, has_side_effects=True, vmem_limit_bytes=60 * 2**20),
    )(row_ptr, col_idx, regime, adjoint, blocks, jac)


def solution(mesh):
    return jax.shard_map(
        functools.partial(body, n_cells=mesh.shape["cells"], n_tracer=mesh.shape["tracer"]),
        mesh=mesh,
        in_specs=(
            P("tracer", "cells"),
            P("cells", None, None),
            P("cells", None),
            P("cells"),
            P("cells"),
            P(),
        ),
        out_specs=P("tracer", "cells"),
        check_vma=False,
    )
```

```python
import functools
import math

import jax
import jax.numpy as jnp
from jax import lax
from jax.experimental import pallas as pl
from jax.experimental.pallas import tpu as pltpu
from jax.sharding import PartitionSpec as P

BLOCK = 128
STEPS = 2
KMAX = 4
CHUNKS = 8
UNROLL = 4
PIECES = 2
HALO = 4


def split(v):
    high = v.astype(jnp.bfloat16).astype(jnp.float32)
    return high, v - high


def kernel(n_cells, n_tracer, row_ptr_hbm, col_idx_hbm, regime_hbm, adjoint, blocks, jac_hbm, out,
           row_ptr, col_idx, regime, jac, raw, weights, jt, ext, halves, sent, arrived, back,
           raw_sem, near_sem, first_send, first_recv, to_send, to_recv,
           back_send, back_recv, halo_send, halo_recv, out_sem, small_sem):
    spec, cells = adjoint.shape
    slots = blocks.shape[0]
    nb = cells // BLOCK
    rows = nb // n_tracer
    part = cells // n_tracer
    nb_total = nb * n_cells
    pieces = arrived.shape[1]
    piece = part // pieces
    piece_rows = rows // pieces
    d = lax.axis_index("cells")
    t = lax.axis_index("tracer")
    right = lax.rem(d + 1, n_cells)
    left = lax.rem(d + n_cells - 1, n_cells)

    per = slots // CHUNKS
    raw_copies = [
        pltpu.make_async_copy(blocks.at[pl.ds(c * per, per)], raw.at[pl.ds(c * per, per)], raw_sem.at[c])
        for c in range(CHUNKS)
    ]

    barrier = pltpu.get_barrier_semaphore()
    pl.semaphore_signal(barrier, inc=1, device_id={"cells": left}, device_id_type=pl.DeviceIdType.MESH)
    pl.semaphore_signal(barrier, inc=1, device_id={"cells": right}, device_id_type=pl.DeviceIdType.MESH)
    for p in range(1, n_tracer):
        pl.semaphore_signal(barrier, inc=1, device_id={"tracer": lax.rem(t + p, n_tracer)},
                            device_id_type=pl.DeviceIdType.MESH)
    near = pltpu.make_async_copy(adjoint, ext.at[0, :, pl.ds(cells, cells)], near_sem)
    near.start()
    small = [
        pltpu.make_async_copy(source, here, small_sem.at[i])
        for i, (source, here) in enumerate(
            ((row_ptr_hbm, row_ptr), (col_idx_hbm, col_idx), (regime_hbm, regime), (jac_hbm, jac)))
    ]
    for copy in small:
        copy.start()
    pl.semaphore_wait(barrier, n_tracer + 1)

    def remote(src, dst, send, recv, where):
        return pltpu.make_async_remote_copy(
            src_ref=src, dst_ref=dst, send_sem=send, recv_sem=recv,
            device_id=where, device_id_type=pl.DeviceIdType.MESH)

    near.wait()
    wide = cells // HALO
    first = [
        remote(ext.at[0, :, pl.ds(cells + g * wide, wide)], ext.at[0, :, pl.ds(third * cells + g * wide, wide)],
               first_send.at[side, g], first_recv.at[side, g], {"cells": where})
        for g in range(HALO) for side, (third, where) in enumerate(((0, right), (2, left)))
    ]
    for copy in first:
        copy.start()
    for copy in raw_copies:
        copy.start()

    for copy in small:
        copy.wait()
    for r in range(jac.shape[0]):
        high, low = split(jnp.transpose(jac[r]))
        jt[r] = jnp.concatenate([high, low], axis=0).astype(jnp.bfloat16)
    for c in range(CHUNKS):
        raw_copies[c].wait()

        def prepare(s, carry):
            high, low = split(raw[s])
            weights[s, 0:BLOCK] = high.astype(jnp.bfloat16)
            weights[s, BLOCK:2 * BLOCK] = low.astype(jnp.bfloat16)
            return carry

        lax.fori_loop(c * per, (c + 1) * per, prepare, 0, unroll=2)

    def take_in(step, begin, count):
        def one(i, carry):
            g = begin + i
            high, low = split(ext[step, :, pl.ds(pl.multiple_of(g * BLOCK, BLOCK), BLOCK)])
            halves[g] = jnp.concatenate([high, low], axis=0).astype(jnp.bfloat16)
            return carry

        lax.fori_loop(0, count, one, 0, unroll=min(UNROLL, count))

    halves[3 * nb] = jnp.zeros((2 * spec, BLOCK), jnp.bfloat16)
    take_in(0, nb, nb)
    for i, copy in enumerate(first):
        copy.wait_recv()
        take_in(0, (i % 2) * 2 * nb + (i // 2) * (nb // HALO), nb // HALO)

    def moved_row(row):
        begin = row_ptr[0, row]
        end = row_ptr[0, row + 1]
        xs, ws = [], []
        for k in range(KMAX):
            live = begin + k < end
            slot = jnp.minimum(begin + k, slots - 1)
            column = col_idx[slot] - (d - 1) * nb
            column = jnp.where(column < 0, column + nb_total, column)
            column = jnp.where(column >= nb_total, column - nb_total, column)
            column = jnp.where(live, jnp.clip(column, 0, 3 * nb - 1), 3 * nb)
            xs.append(halves[column])
            ws.append(weights[slot])
        lhs = jnp.concatenate(xs, axis=1)
        got = lax.dot_general(lhs, jnp.concatenate(ws, axis=1), (((1,), (1,)), ((), ())),
                              preferred_element_type=jnp.float32)
        got = got[:, 0:BLOCK] + got[:, BLOCK:2 * BLOCK]
        return got[0:spec] + got[spec:2 * spec]

    pending = list(first)
    peers = range(1, n_tracer)
    for step in range(STEPS):
        to = {}
        for h in range(pieces):
            for p in (*peers, 0):
                owner = lax.rem(t + p, n_tracer)

                def transport(i, carry, p=p, h=h, owner=owner):
                    y = moved_row(owner * rows + h * piece_rows + i)
                    where = pl.ds(pl.multiple_of(i * BLOCK, BLOCK), BLOCK)
                    if p:
                        sent[step, h, p, :, where] = y
                    else:
                        arrived[step, h, t, :, where] = y
                    return carry

                lax.fori_loop(0, piece_rows, transport, 0, unroll=min(UNROLL, piece_rows))
                if p:
                    to[h, p] = remote(sent.at[step, h, p], arrived.at[step, h, t], to_send.at[step, h, p],
                                      to_recv.at[step, h, p], {"tracer": owner})
                    to[h, p].start()

        last = step == STEPS - 1
        returned, halo = {}, []

        def place(third, q, h):
            start = third * cells + q * part + h * piece
            return ext.at[step + 1, :, pl.ds(pl.multiple_of(start, BLOCK), piece)]

        def forward(p, h):
            q = lax.rem(t + n_tracer - p, n_tracer)
            for side, (third, where) in enumerate(((0, right), (2, left))):
                copy = remote(place(1, q, h), place(third, q, h), halo_send.at[step, side, h, p],
                              halo_recv.at[step, side, h, p], {"cells": where})
                copy.start()
                halo.append((copy, third * nb + q * rows + h * piece_rows))

        for h in range(pieces):
            for p in peers:
                to[h, p].wait_recv()
            for b in range(piece_rows):
                cols = pl.ds(b * BLOCK, BLOCK)
                m = jnp.concatenate([arrived[step, h, q, :, cols] for q in range(n_tracer)], axis=0)
                high, low = split(m)
                got = lax.dot_general(jt[regime[t * rows + h * piece_rows + b]],
                                      jnp.concatenate([high, low], axis=1).astype(jnp.bfloat16),
                                      (((1,), (0,)), ((), ())), preferred_element_type=jnp.float32)
                got = got[:, 0:BLOCK] + got[:, BLOCK:2 * BLOCK]
                half = got.shape[0] // 2
                got = got[0:half] + got[half:]
                for q in range(n_tracer):
                    back[step, h, q, :, cols] = got[q * spec:(q + 1) * spec]

            mine = pl.ds(pl.multiple_of(t * part + h * piece, BLOCK), piece)
            for p in peers:
                q = lax.rem(t + p, n_tracer)
                target = out.at[:, mine] if last else place(1, t, h)
                returned[h, p] = remote(back.at[step, h, q], target, back_send.at[step, h, p],
                                        back_recv.at[step, h, p], {"tracer": q})
                returned[h, p].start()
            if last:
                pltpu.make_async_copy(back.at[step, h, t], out.at[:, mine], out_sem.at[h]).start()
            else:
                ext[step + 1, :, pl.ds(pl.multiple_of(cells + t * part + h * piece, BLOCK), piece)] = back[step, h, t]
                forward(0, h)
        for h in range(pieces):
            for p in peers:
                returned[h, p].wait_recv()
                if not last:
                    forward(p, h)
            if last:
                mine = pl.ds(pl.multiple_of(t * part + h * piece, BLOCK), piece)
                pltpu.make_async_copy(back.at[step, h, t], out.at[:, mine], out_sem.at[h]).wait()
        if not last:
            take_in(step + 1, nb, nb)
        for copy, begin in halo:
            copy.wait_recv()
            take_in(step + 1, begin, piece_rows)
        pending += [*to.values(), *returned.values(), *(copy for copy, _ in halo)]
    for copy in pending:
        copy.wait_send()


def body(adjoint, blocks, row_ptr, col_idx, regime, jac, n_cells, n_tracer):
    spec, cells = adjoint.shape
    slots = blocks.shape[0]
    part = cells // n_tracer
    pieces = math.gcd(PIECES, part // BLOCK)
    f32, bf16 = jnp.float32, jnp.bfloat16
    dma = pltpu.SemaphoreType.DMA
    return pl.pallas_call(
        functools.partial(kernel, n_cells, n_tracer),
        out_shape=jax.ShapeDtypeStruct((spec, cells), f32),
        in_specs=[pl.BlockSpec(memory_space=pl.ANY)] * 6,
        out_specs=pl.BlockSpec(memory_space=pl.ANY),
        scratch_shapes=[
            pltpu.SMEM(row_ptr.shape, row_ptr.dtype),
            pltpu.SMEM(col_idx.shape, col_idx.dtype),
            pltpu.SMEM(regime.shape, regime.dtype),
            pltpu.VMEM(jac.shape, f32),
            pltpu.VMEM((slots, BLOCK, BLOCK), f32),
            pltpu.VMEM((slots, 2 * BLOCK, BLOCK), bf16),
            pltpu.VMEM((jac.shape[0], 2 * jac.shape[2], jac.shape[1]), bf16),
            pltpu.VMEM((STEPS, spec, 3 * cells), f32),
            pltpu.VMEM((3 * cells // BLOCK + 1, 2 * spec, BLOCK), bf16),
            pltpu.VMEM((STEPS, pieces, n_tracer, spec, part // pieces), f32),
            pltpu.VMEM((STEPS, pieces, n_tracer, spec, part // pieces), f32),
            pltpu.VMEM((STEPS, pieces, n_tracer, spec, part // pieces), f32),
            dma((CHUNKS,)), dma(()), dma((2, HALO)), dma((2, HALO)),
            dma((STEPS, pieces, n_tracer)), dma((STEPS, pieces, n_tracer)),
            dma((STEPS, pieces, n_tracer)), dma((STEPS, pieces, n_tracer)),
            dma((STEPS, 2, pieces, n_tracer)), dma((STEPS, 2, pieces, n_tracer)), dma((pieces,)), dma((4,)),
        ],
        compiler_params=pltpu.CompilerParams(
            collective_id=0, has_side_effects=True, vmem_limit_bytes=60 * 2**20),
    )(row_ptr, col_idx, regime, adjoint, blocks, jac)


def solution(mesh):
    return jax.shard_map(
        functools.partial(body, n_cells=mesh.shape["cells"], n_tracer=mesh.shape["tracer"]),
        mesh=mesh,
        in_specs=(
            P("tracer", "cells"),
            P("cells", None, None),
            P("cells", None),
            P("cells"),
            P("cells"),
            P(),
        ),
        out_specs=P("tracer", "cells"),
        check_vma=False,
    )
```
